512 devices in a mesh: row: 32 (over y, z_hi), col: 16 (over x, z_lo, core).
Axes of the slice: x: 4, y: 8, z: 8 (z_hi: 4, z_lo: 2; z = z_hi * 2 + z_lo), core: 2. Of those that a mesh axis runs over, the one named last changes fastest.
Arguments:
- features: bfloat16 [65536, 128], P(('row', 'col')), may hold values from -6 to 6
- adj_tiles: bfloat16 [49152, 128, 128], P(('row', 'col')), may hold values from -1 to 1
- tile_dest: int32 [49152], P(('row', 'col')), may hold values from 0 to 15
- tile_src: int32 [49152], P(('row', 'col')), may hold values from 0 to 31
- live_tiles: int32 [512], P(('row', 'col')), may hold values from 1 to 96, as said below
- degrees: int32 [65536], P(('row', 'col')), may hold values from 8 to 64
- self_one: bfloat16 [128, 256], replicated, may hold values from -0.5 to 0.5
- neigh_one: bfloat16 [128, 256], replicated, may hold values from -0.5 to 0.5
- bias_one: float32 [256], replicated, may hold values from -3 to 3
- self_two: bfloat16 [256, 256], replicated, may hold values from -0.375 to 0.375
- neigh_two: bfloat16 [256, 256], replicated, may hold values from -0.375 to 0.375
- bias_two: float32 [256], replicated, may hold values from -3 to 3
Outputs:
- embeddings: bfloat16 [65536, 256], P(('row', 'col'))
The draws below stay inside these ranges and needn't reach their ends.
Inputs may be any that keep to these rules, and one draw needn't show every extreme that they name: `live_tiles`: slots at or above a device's count are not part of the adjacency. Some device has all 96 slots live.
All inputs are finite; a program needn't handle non-finite values.
Results may differ from the reference program's by a relative error of at most 0.018.
Values may be sent and summed in bfloat16 or wider, within the bound.
A program may use at most 64 MiB of HBM per device.

```python
import jax
import jax.numpy as jnp
from jax import lax

F_IN = 128
HID = 256
NODE_DEV = 128
SLOTS = 96
NODES = 65536
N_ROW = 32
N_COL = 16


def draw_live_tiles(key, part):
    key = jax.random.fold_in(key, 11)
    first_key, second_key = jax.random.split(key)
    device_total = N_ROW * N_COL
    counts = jax.random.randint(first_key, (device_total,), max(1, SLOTS // 8), SLOTS // 2 + 1, dtype=jnp.int32)
    busiest = jax.random.randint(second_key, (), 0, device_total, dtype=jnp.int32)
    device_index = jnp.arange(device_total, dtype=jnp.int32)
    return jnp.where(device_index == busiest, SLOTS, counts).astype(jnp.int32)


def with_ends(entries, stream_key, least, top_value):
    index_at = [jax.random.randint(jax.random.fold_in(stream_key, axis), (), 0, length) for axis, length in enumerate(entries.shape)]
    longest = entries.shape.index(max(entries.shape))
    next_to = index_at[:longest] + [(index_at[longest] + 1) % entries.shape[longest]] + index_at[longest + 1:]
    return entries.at[tuple(index_at)].set(least).at[tuple(next_to)].set(top_value)


def steps_of(own_key, extent, cuts, smallest, high):
    loudness, own = 1.0, jax.random.fold_in(own_key, 6)
    for dim, parts in cuts:
        steps = jnp.exp(jax.random.uniform(jax.random.fold_in(own, dim), (parts,), jnp.float32, smallest / len(cuts), high / len(cuts)))
        loudness = loudness * jnp.repeat(steps, extent[dim] // parts).reshape([-1 if axis == dim else 1 for axis in range(len(extent))])
    return loudness


def bell_draw(rng, dims, deviation, reach, pieces=(), held_as=jnp.bfloat16):
    drawn = deviation * jax.random.normal(rng, dims, jnp.float32)
    if pieces:
        drawn = drawn * steps_of(rng, dims, pieces, -0.22, 0.18)
    return jnp.clip(drawn, -reach, reach).astype(held_as)


def setup_inputs(seed: int = 0) -> dict:
    seeds = jax.random.split(jax.random.key(seed), 13)
    return {
        "features": bell_draw(seeds[0], (NODES, F_IN), 1.0, 6.0, ((0, 512),)),
        "adj_tiles": jnp.clip(jax.random.uniform(seeds[1], (N_ROW * N_COL * SLOTS, 128, 128), jnp.float32, -1.0, 1.0) * steps_of(seeds[1], (N_ROW * N_COL * SLOTS, 128, 128), ((0, 512),), -0.4, 0.0), -1.0, 1.0).astype(jnp.bfloat16),
        "tile_dest": with_ends(jax.random.randint(seeds[2], (N_ROW * N_COL * SLOTS,), 0, N_COL * NODE_DEV // 128), jax.random.fold_in(seeds[2], 1), 0, (N_COL * NODE_DEV // 128) - 1).astype(jnp.int32),
        "tile_src": with_ends(jax.random.randint(seeds[3], (N_ROW * N_COL * SLOTS,), 0, N_ROW * NODE_DEV // 128), jax.random.fold_in(seeds[3], 1), 0, (N_ROW * NODE_DEV // 128) - 1).astype(jnp.int32),
        "live_tiles": draw_live_tiles(jax.random.fold_in(seeds[12], 71), 0),
        "degrees": with_ends(jax.random.randint(seeds[5], (NODES,), 8, 65), jax.random.fold_in(seeds[5], 1), 8, 64).astype(jnp.int32),
        "self_one": bell_draw(seeds[6], (F_IN, HID), F_IN ** -0.5, 0.5),
        "neigh_one": bell_draw(seeds[7], (F_IN, HID), F_IN ** -0.5, 0.5),
        "bias_one": bell_draw(seeds[8], (HID,), 0.5, 3.0, (), jnp.float32),
        "self_two": bell_draw(seeds[9], (HID, HID), HID ** -0.5, 0.375),
        "neigh_two": bell_draw(seeds[10], (HID, HID), HID ** -0.5, 0.375),
        "bias_two": bell_draw(seeds[11], (HID,), 0.5, 3.0, (), jnp.float32),
    }


def normalize_relu(pre_values):
    positive = jnp.maximum(pre_values, 0.0)
    mean_square = lax.optimization_barrier(jnp.mean(positive * positive, axis=-1, keepdims=True))
    return (positive * lax.rsqrt(mean_square + 1e-05)).astype(jnp.bfloat16)

def aggregate(node_rows, adj_tiles, tile_dest, tile_src, live_tiles, round_partial):
    feat_width = node_rows.shape[1]
    tile_rows = NODE_DEV // 128
    dest_count = N_COL * tile_rows
    group_rows = N_COL * NODE_DEV
    device_total = N_ROW * N_COL
    grouped = node_rows.reshape(N_ROW, N_COL, NODE_DEV, feat_width)
    tiles_all = adj_tiles.reshape(device_total, SLOTS, 128, 128)
    dest_all = tile_dest.reshape(device_total, SLOTS)
    src_all = tile_src.reshape(device_total, SLOTS)
    positions = jnp.arange(dest_count, dtype=jnp.int32)
    slot_index = jnp.arange(SLOTS, dtype=jnp.int32)

    def per_device(totals, inputs):
        device, tiles_here, dest_here, src_here, live_here = inputs
        column = device % N_COL
        grid_row = device // N_COL
        sources = lax.dynamic_index_in_dim(grouped, column, axis=1, keepdims=False)
        sources = sources.reshape(N_ROW * tile_rows, 128, feat_width).astype(jnp.float32)
        picked = jnp.take(sources, src_here, axis=0)
        products = jnp.einsum('sij,sjw->siw', tiles_here.astype(jnp.float32), picked, precision=lax.Precision.HIGHEST)
        is_live = slot_index < live_here
        onehot = jnp.where(is_live[:, None] & (dest_here[:, None] == positions[None, :]), 1.0, 0.0).astype(jnp.float32)
        partial_value = jnp.einsum('sn,siw->niw', onehot, products, precision=lax.Precision.HIGHEST)
        partial_value = partial_value.reshape(group_rows, feat_width)
        if round_partial:
            partial_value = lax.optimization_barrier(partial_value.astype(jnp.bfloat16)).astype(jnp.float32)
        row_start = (grid_row * group_rows).astype(jnp.int32)
        current = lax.dynamic_slice_in_dim(totals, row_start, group_rows, 0)
        totals = lax.dynamic_update_slice_in_dim(totals, current + partial_value, row_start, 0)
        return (totals, None)
    devices = jnp.arange(device_total, dtype=jnp.int32)
    initial = jnp.zeros((NODES, feat_width), jnp.float32)
    totals, _ = lax.scan(per_device, initial, (devices, tiles_all, dest_all, src_all, live_tiles))
    return totals

def reference(features, adj_tiles, tile_dest, tile_src, live_tiles, degrees, self_one, neigh_one, bias_one, self_two, neigh_two, bias_two):
    divisor = degrees.astype(jnp.float32)[:, None]
    first = aggregate(features, adj_tiles, tile_dest, tile_src, live_tiles, False) / divisor
    pre_one = jnp.dot(features, self_one, preferred_element_type=jnp.float32)
    pre_one = pre_one + jnp.dot(first, neigh_one.astype(jnp.float32), precision=lax.Precision.HIGHEST)
    pre_one = pre_one + bias_one.astype(jnp.float32)
    hidden = normalize_relu(pre_one)
    second = aggregate(hidden, adj_tiles, tile_dest, tile_src, live_tiles, True) / divisor
    pre_two = jnp.dot(hidden, self_two, preferred_element_type=jnp.float32)
    pre_two = pre_two + jnp.dot(second, neigh_two.astype(jnp.float32), precision=lax.Precision.HIGHEST)
    pre_two = pre_two + bias_two.astype(jnp.float32)
    return normalize_relu(pre_two)
```

```python
import jax
import jax.numpy as jnp
from jax import lax
from jax.experimental import pallas as pl
from jax.experimental.pallas import tpu as pltpu
from jax.sharding import PartitionSpec as P

NY, NZ = 8, 4
NX, NL, NC = 4, 2, 2
B = 128
SLOTS = 96
NDEST = NX * NL * NC
BF, F32, I32 = jnp.bfloat16, jnp.float32, jnp.int32
MESH = pl.DeviceIdType.MESH
X_ORDER = (2, 1, 3, 0)
LAG = 2


def mod(value, size):
    return lax.rem(value + size, jnp.int32(size))


def relu_norm(pre):
    positive = jnp.maximum(pre, 0.0)
    mean_square = jnp.mean(positive * positive, axis=-1, keepdims=True)
    return (positive * lax.rsqrt(mean_square + 1e-05)).astype(BF)


def mm(a, b):
    return jnp.dot(a, b, preferred_element_type=F32)


def mm_split(a, b):
    high = a.astype(BF)
    low = (a - high.astype(F32)).astype(BF)
    return mm(high, b) + mm(low, b)


def kernel(
    features, tiles, dest, src, live, degrees, w_self1, w_neigh1, bias1, w_self2, w_neigh2, bias2,
    out,
    xg, adj, tile_in, tile_f, tile_b, acc, send1, recv1, send2, recv2, tab_v, tab_s,
    ws1, wn1, ws2, wn2, divisor, self_part,
    load_sem, zs, zr, ys, yr, s1s, s1r, s2s, s2r,
):
    row, col = lax.axis_index("row"), lax.axis_index("col")
    y, z = lax.div(row, jnp.int32(NZ)), lax.rem(row, jnp.int32(NZ))
    x = lax.div(col, jnp.int32(NL * NC))
    zl = lax.rem(lax.div(col, jnp.int32(NC)), jnp.int32(NL))
    core = lax.rem(col, jnp.int32(NC))

    def at_y(dy):
        return (mod(y + dy, NY) * NZ + z, col)

    def at_z(dz):
        return (y * NZ + mod(z + dz, NZ), col)

    def at_xl(dx, dl):
        return (row, (mod(x + dx, NX) * NL + mod(zl + dl, NL)) * NC + core)

    other_core = (row, col + 1 - 2 * core)

    load_features = pltpu.make_async_copy(features, xg.at[0, y, z], load_sem.at[0])
    load_tiles = pltpu.make_async_copy(tiles, tile_in, load_sem.at[1])
    weight_loads = [
        pltpu.make_async_copy(a, b, load_sem.at[3 + i])
        for i, (a, b) in enumerate(((w_self1, ws1), (w_neigh1, wn1), (w_self2, ws2), (w_neigh2, wn2)))
    ]
    load_features.start()
    load_tiles.start()
    for load in weight_loads:
        load.start()

    barrier = pltpu.get_barrier_semaphore()
    partners = [at_y(1), at_y(-1)]
    partners += [at_z(dz) for dz in range(1, NZ)]
    partners += [at_xl(dx, dl) for dx in range(NX) for dl in range(NL) if dx or dl]
    partners += [other_core]
    for partner in partners:
        pl.semaphore_signal(barrier, inc=1, device_id=partner, device_id_type=MESH)
    pl.semaphore_wait(barrier, len(partners))

    def remote(a, b, ss, rs, device):
        return pltpu.make_async_remote_copy(
            src_ref=a, dst_ref=b, send_sem=ss, recv_sem=rs, device_id=device, device_id_type=MESH
        )

    started = []

    def send(a, b, ss, rs, device):
        copy = remote(a, b, ss, rs, device)
        copy.start()
        started.append(copy)

    def z_send(p):
        for dz in (1, 3, 2):
            ref = xg.at[p, y, z]
            send(ref, ref, zs.at[p, dz - 1], zr.at[p, dz - 1], at_z(dz))

    def piece(p, k, way, dz):
        return xg.at[p, mod(y - k if way == 0 else y + k, NY), mod(z - dz, NZ)]

    def carries(k, way, dz):
        return k < NY // 2 or (dz < NZ // 2) == (way == 0)

    def forward(p, k, way, dz):
        if k + 1 <= NY // 2 and carries(k + 1, way, dz):
            ref = piece(p, k, way, dz)
            send(ref, ref, ys.at[p, way, k, dz], yr.at[p, way, k, dz], at_y(1 if way == 0 else -1))

    def wait_piece(p, k, way, dz):
        ref = piece(p, k, way, dz)
        remote(ref, ref, ys.at[p, way, k - 1, dz], yr.at[p, way, k - 1, dz], at_y(-1 if way == 0 else 1)).wait_recv()

    def step(p, k):
        for dz in (0, 1, 3, 2):
            if k == 0:
                if dz:
                    ref = xg.at[p, y, mod(z - dz, NZ)]
                    remote(ref, ref, zs.at[p, dz - 1], zr.at[p, dz - 1], at_z(-dz)).wait_recv()
                for way in (0, 1):
                    forward(p, 0, way, dz)
            else:
                for way in (0, 1):
                    if carries(k, way, dz):
                        wait_piece(p, k, way, dz)
                        forward(p, k, way, dz)

    def bundles(k):
        if k == 0:
            return [y]
        if k == NY // 2:
            return [mod(y + k, NY)]
        return [mod(y - k, NY), mod(y + k, NY)]

    def product(p, k, block_x):
        total = None
        for b in bundles(k):
            lhs = adj[b, pl.ds(block_x * (NL * NC), NL * NC)].reshape(NL * NC * B, NZ * B)
            part = mm(lhs, xg[p, b].reshape(NZ * B, B))
            total = part if total is None else total + part
        return total.reshape(NL * NC, B, B)

    def compute(p, k):
        @pl.loop(0, NX)
        def _(block_x):
            rows = pl.ds(block_x * (NL * NC), NL * NC)
            value = product(p, k, block_x)
            if k:
                value = value + acc[p, rows]
            acc[p, rows] = value

    def dest_block(dx, dl, c):
        return (mod(x + dx, NX) * NL + mod(zl + dl, NL)) * NC + c

    def finish_and_exchange(p):
        for i, dx in enumerate(X_ORDER):
            block_x = mod(x + dx, NX)
            rows = pl.ds(block_x * (NL * NC), NL * NC)
            acc[p, rows] = product(p, NY // 2, block_x) + acc[p, rows]
            for dl in range(NL):
                send1[p, i, dl] = acc[p, dest_block(dx, dl, 1 - core)].astype(BF)
            send(send1.at[p, i], recv1.at[p, i], s1s.at[p, i], s1r.at[p, i], other_core)

    def scatter(p):
        for i, dx in enumerate(X_ORDER):
            remote(send1.at[p, i], recv1.at[p, i], s1s.at[p, i], s1r.at[p, i], other_core).wait_recv()
            for dl in (1, 0):
                d = dest_block(dx, dl, core)
                value = acc[p, d] + recv1[p, i, dl].astype(F32)
                if dx or dl:
                    j = dx * NL + dl - 1
                    send2[p, j] = value.astype(BF)
                    send(send2.at[p, j], recv2.at[p, j], s2s.at[p, j], s2r.at[p, j], at_xl(dx, dl))
                else:
                    acc[p, d] = value

    def collect(p):
        total = acc[p, dest_block(0, 0, core)]
        for j in range(NX * NL - 1):
            dx, dl = divmod(j + 1, NL)
            remote(send2.at[p, j], recv2.at[p, j], s2s.at[p, j], s2r.at[p, j], at_xl(-dx, -dl)).wait_recv()
            total = total + recv2[p, j].astype(F32)
        return total / divisor[...]

    load_features.wait()
    z_send(0)
    for way in (0, 1):
        forward(0, 0, way, 0)

    lane = lax.broadcasted_iota(I32, (1, B), 1)
    tab_v[...] = jnp.zeros_like(tab_v)
    tab_v[0:1, 0:SLOTS] = dest[...]
    tab_v[1:2, 0:SLOTS] = src[...]
    place = jnp.where(lane < live[0], tab_v[1:2, :] * NDEST + tab_v[0:1, :], -1)
    place_j = jnp.broadcast_to(place, (B, B)).T
    slot_j = lax.broadcasted_iota(I32, (B, B), 0)
    lanes = lax.broadcasted_iota(I32, (B, B), 1)

    def lowest(mask):
        return jnp.min(jnp.where(mask, slot_j, SLOTS), axis=0, keepdims=True)

    for i in range(NY * NZ * NDEST // B):
        tab_v[i : i + 1, :] = lowest(place_j == lanes + i * B)
    tab_v[4:5, :] = lowest((place_j == place) & (slot_j > lanes) & (place >= 0))
    load_table = pltpu.make_async_copy(tab_v, tab_s, load_sem.at[2])
    load_table.start()
    divisor[...] = jnp.broadcast_to(degrees[...].astype(F32), (B, B)).T
    load_table.wait()
    load_tiles.wait()

    def slot_at(i, j):
        return lax.clamp(jnp.int32(0), tab_s[i, j], jnp.int32(SLOTS))

    tile_f[SLOTS] = jnp.zeros((B, B), F32)
    tile_b[SLOTS] = jnp.zeros((B, B), BF)

    @pl.loop(0, SLOTS)
    def _(i):
        slot = SLOTS - 1 - i
        value = tile_in[slot].astype(F32) + tile_f[slot_at(4, slot)]
        tile_f[slot] = value
        tile_b[slot] = value.astype(BF)

    def build(k):
        for b in bundles(k):
            @pl.loop(0, NDEST)
            def _(d):
                for zz in range(NZ):
                    entry = b * (NZ * NDEST) + zz * NDEST + d
                    slot = slot_at(lax.div(entry, jnp.int32(B)), lax.rem(entry, jnp.int32(B)))
                    adj[b, d, :, zz * B : (zz + 1) * B] = tile_b[slot]

    for k in range(NY // 2):
        if k == 0:
            for dz in (1, 3, 2):
                ref = xg.at[0, y, mod(z - dz, NZ)]
                remote(ref, ref, zs.at[0, dz - 1], zr.at[0, dz - 1], at_z(-dz)).wait_recv()
                for way in (0, 1):
                    forward(0, 0, way, dz)
        else:
            step(0, k)
        build(k)
        compute(0, k)
    build(NY // 2)
    for load in weight_loads:
        load.wait()
    own = xg[0, y, z]
    self_part[...] = mm(own, ws1[...]) + bias1[...]
    step(0, NY // 2)
    finish_and_exchange(0)
    scatter(0)
    first = collect(0)
    hidden = relu_norm(self_part[...] + mm_split(first, wn1[...]))
    xg[1, y, z] = hidden[:, :B]
    xg[2, y, z] = hidden[:, B:]

    z_send(1)
    z_send(2)
    last = NY // 2
    for t in range(last + LAG + 1):
        if t <= last:
            step(1, t)
        if 0 <= t - LAG <= last:
            step(2, t - LAG)
        if t == 0:
            self_part[...] = mm(hidden, ws2[...]) + bias2[...]
        if t < last:
            compute(1, t)
        if t == last:
            finish_and_exchange(1)
        if t == last + 1:
            scatter(1)
        if t == last + 2:
            self_part[...] += mm_split(collect(1), wn2[0:B, :])
        if 0 <= t - LAG < last:
            compute(2, t - LAG)
    finish_and_exchange(2)
    scatter(2)
    out[...] = relu_norm(self_part[...] + mm_split(collect(2), wn2[B:, :]))
    for copy in started:
        copy.wait_send()


def shards(
    features, adj_tiles, tile_dest, tile_src, live_tiles, degrees,
    self_one, neigh_one, bias_one, self_two, neigh_two, bias_two,
):
    hid = self_one.shape[1]
    any_spec = pl.BlockSpec(memory_space=pl.ANY)
    vmem_spec = pl.BlockSpec(memory_space=pltpu.VMEM)
    smem_spec = pl.BlockSpec(memory_space=pltpu.SMEM)
    sem = pltpu.SemaphoreType.DMA
    return pl.pallas_call(
        kernel,
        out_shape=jax.ShapeDtypeStruct((B, hid), BF),
        in_specs=[
            any_spec, any_spec, vmem_spec, vmem_spec, smem_spec, vmem_spec,
            any_spec, any_spec, vmem_spec, any_spec, any_spec, vmem_spec,
        ],
        out_specs=vmem_spec,
        scratch_shapes=[
            pltpu.VMEM((3, NY, NZ, B, B), BF),
            pltpu.VMEM((NY, NDEST, B, NZ * B), BF),
            pltpu.VMEM((SLOTS, B, B), BF),
            pltpu.VMEM((SLOTS + 1, B, B), F32),
            pltpu.VMEM((SLOTS + 1, B, B), BF),
            pltpu.VMEM((3, NDEST, B, B), F32),
            pltpu.VMEM((3, NX, NL, B, B), BF),
            pltpu.VMEM((3, NX, NL, B, B), BF),
            pltpu.VMEM((3, NX * NL - 1, B, B), BF),
            pltpu.VMEM((3, NX * NL - 1, B, B), BF),
            pltpu.VMEM((8, B), I32),
            pltpu.SMEM((8, B), I32),
            pltpu.VMEM((B, hid), BF),
            pltpu.VMEM((B, hid), BF),
            pltpu.VMEM((hid, hid), BF),
            pltpu.VMEM((hid, hid), BF),
            pltpu.VMEM((B, B), F32),
            pltpu.VMEM((B, hid), F32),
            sem((7,)),
            sem((3, NZ - 1)),
            sem((3, NZ - 1)),
            sem((3, 2, NY // 2, NZ)),
            sem((3, 2, NY // 2, NZ)),
            sem((3, NX)),
            sem((3, NX)),
            sem((3, NX * NL - 1)),
            sem((3, NX * NL - 1)),
        ],
        compiler_params=pltpu.CompilerParams(
            collective_id=0, has_side_effects=True, vmem_limit_bytes=56 * 1024 * 1024
        ),
    )(
        features, adj_tiles, tile_dest[None], tile_src[None], live_tiles, degrees[None],
        self_one, neigh_one, bias_one[None], self_two, neigh_two, bias_two[None],
    )


def solution(mesh):
    rows = P(("row", "col"))
    in_specs = (rows,) * 6 + (P(),) * 6
    return jax.shard_map(shards, mesh=mesh, in_specs=in_specs, out_specs=rows, check_vma=False)
```
